256 devices in a mesh: group: 32 (over z, y_hi, core), seq: 8 (over x, y_lo).
Axes of the slice: x: 4, y: 4 (y_hi: 2, y_lo: 2; y = y_hi * 2 + y_lo), z: 8, core: 2. Of those that a mesh axis runs over, the one named last changes fastest.
Arguments:
- spatial_qkv: bfloat16 [32, 8, 512, 4608], P('group', 'seq'), may hold values from -6 to 6
- temporal_qkv: bfloat16 [32, 8, 512, 4608], P('group', 'seq'), may hold values from -6 to 6
- caption_kv: bfloat16 [32, 1024, 3072], P(None, 'group'), may hold values from -6 to 6
- frame_count: int32 [32], P('group'), may hold values from 1 to 8, as said below
- caption_len: int32 [32], P('group'), may hold values from 1 to 1024, as said below
Outputs:
- attn_mix: bfloat16 [32, 8, 512, 1536], P('group', 'seq')
The draws below stay inside these ranges and needn't reach their ends.
Inputs may be any that keep to these rules, and one draw needn't show every extreme that they name: `frame_count`: each video has 1 to 8 frames with data, the first ones; some video has all 8. `caption_len`: each caption has 1 to 1024 tokens with data, the first ones; some caption has all 1024.
All inputs are finite; a program needn't handle non-finite values.
Results may differ from the reference program's by a relative error of at most 0.012.
Values may be sent and summed in bfloat16 or wider, within the bound.
A program may use at most 192 MiB of HBM per device.

```python
import jax
import jax.numpy as jnp
from jax import lax

HEADS = 12
HD = 128
S = 512
FRAMES = 8
CAP = 1024
VIDEOS = 32


def draw_spatial_qkv(key, part):
    key = jax.random.fold_in(key, 5)
    feat_width = HEADS * HD
    shape = (VIDEOS, FRAMES, S, 3 * feat_width)
    return jnp.clip(jax.random.normal(key, shape, jnp.float32), -6.0, 6.0).astype(jnp.bfloat16)


def draw_temporal_qkv(key, part):
    key = jax.random.fold_in(key, 7)
    feat_width = HEADS * HD
    shape = (VIDEOS, FRAMES, S, 3 * feat_width)
    return jnp.clip(jax.random.normal(key, shape, jnp.float32), -6.0, 6.0).astype(jnp.bfloat16)


def draw_caption_kv(key, part):
    key = jax.random.fold_in(key, 9)
    feat_width = HEADS * HD
    shape = (VIDEOS, CAP, 2 * feat_width)
    return jnp.clip(jax.random.normal(key, shape, jnp.float32), -6.0, 6.0).astype(jnp.bfloat16)


def draw_frame_count(key, part):
    key = jax.random.fold_in(key, 11)
    first_key, second_key = jax.random.split(key)
    counts = jax.random.randint(first_key, (VIDEOS,), 1, FRAMES + 1)
    longest = jax.random.randint(second_key, (), 0, VIDEOS)
    return jnp.where(jnp.arange(VIDEOS) == longest, FRAMES, counts).astype(jnp.int32)


def draw_caption_len(key, part):
    key = jax.random.fold_in(key, 23)
    first_key, second_key = jax.random.split(key)
    counts = jax.random.randint(first_key, (VIDEOS,), 1, CAP + 1)
    longest = jax.random.randint(second_key, (), 0, VIDEOS)
    return jnp.where(jnp.arange(VIDEOS) == longest, CAP, counts).astype(jnp.int32)


def setup_inputs(seed: int = 0) -> dict:
    seeds = jax.random.split(jax.random.key(seed), 6)
    return {
        "spatial_qkv": draw_spatial_qkv(jax.random.fold_in(seeds[5], 71), 0),
        "temporal_qkv": draw_temporal_qkv(jax.random.fold_in(seeds[5], 71), 0),
        "caption_kv": draw_caption_kv(jax.random.fold_in(seeds[5], 71), 0),
        "frame_count": draw_frame_count(jax.random.fold_in(seeds[5], 71), 0),
        "caption_len": draw_caption_len(jax.random.fold_in(seeds[5], 71), 0),
    }


NEG_FILL = -1e30


def soft_weights(scores):
    row_top = jnp.max(scores, axis=-1, keepdims=True)
    lifted = jnp.exp(scores - row_top)
    return (lifted / jnp.sum(lifted, axis=-1, keepdims=True)).astype(jnp.bfloat16)


def attend(queries, keys_in, values, key_valid):
    scores = jnp.einsum("mhe,khe->hmk", queries.astype(jnp.float32), keys_in.astype(jnp.float32)) * (HD ** -0.5)
    scores = jnp.where(key_valid[None, None, :], scores, NEG_FILL)
    weights = soft_weights(scores)
    return jnp.einsum("hmk,khe->mhe", weights.astype(jnp.float32), values.astype(jnp.float32))


def one_video(packed):
    spatial_rows, temporal_rows, caption_rows, frame_total, caption_total = packed
    feat_width = HEADS * HD
    cap_keys = caption_rows[:, :feat_width].reshape(CAP, HEADS, HD)
    cap_values = caption_rows[:, feat_width:].reshape(CAP, HEADS, HD)
    cap_valid = jnp.arange(CAP) < caption_total
    all_tokens = jnp.ones((S,), dtype=bool)

    def one_frame(frame_rows):
        queries = frame_rows[:, :feat_width].reshape(S, HEADS, HD)
        keys_in = frame_rows[:, feat_width:2 * feat_width].reshape(S, HEADS, HD)
        values = frame_rows[:, 2 * feat_width:].reshape(S, HEADS, HD)
        return attend(queries, keys_in, values, all_tokens) + attend(queries, cap_keys, cap_values, cap_valid)

    local_mix = lax.map(one_frame, spatial_rows)
    t_queries = temporal_rows[..., :feat_width].reshape(FRAMES, S, HEADS, HD).astype(jnp.float32)
    t_keys = temporal_rows[..., feat_width:2 * feat_width].reshape(FRAMES, S, HEADS, HD).astype(jnp.float32)
    t_values = temporal_rows[..., 2 * feat_width:].reshape(FRAMES, S, HEADS, HD).astype(jnp.float32)
    frame_valid = jnp.arange(FRAMES) < frame_total
    scores = jnp.einsum("fphe,gphe->phfg", t_queries, t_keys) * (HD ** -0.5)
    scores = jnp.where(frame_valid[None, None, None, :], scores, NEG_FILL)
    weights = soft_weights(scores)
    temporal_out = jnp.einsum("phfg,gphe->fphe", weights.astype(jnp.float32), t_values).astype(jnp.bfloat16)
    widened = lax.optimization_barrier(temporal_out).astype(jnp.float32)
    mixed = (local_mix + widened) * frame_valid.astype(jnp.float32)[:, None, None, None]
    return mixed.reshape(FRAMES, S, feat_width).astype(jnp.bfloat16)


def reference(spatial_qkv, temporal_qkv, caption_kv, frame_count, caption_len):
    return lax.map(one_video, (spatial_qkv, temporal_qkv, caption_kv, frame_count, caption_len))
```

```python
import functools

import jax
import jax.numpy as jnp
from jax import lax
from jax.experimental import pallas as pl
from jax.experimental.pallas import tpu as pltpu
from jax.sharding import PartitionSpec as P

HD = 128
PAIR = 2 * HD
NEG_FILL = -1e30
LOG2E = 1.4426950408889634
MESH = pl.DeviceIdType.MESH
SETS = 3
ROWS_T = 16
BLOCK = 256


def nt(a, b):
    return lax.dot_general(a, b, (((1,), (1,)), ((), ())), preferred_element_type=jnp.float32)


def soft_apply(scores, values):
    top = jnp.max(scores, axis=-1, keepdims=True)
    lifted = jnp.exp2((scores - top) * (HD ** -0.5 * LOG2E)).astype(jnp.bfloat16)
    wide = jnp.concatenate([values, jnp.ones_like(values)], axis=1)
    mixed = jnp.dot(lifted, wide, preferred_element_type=jnp.float32)
    return mixed[:, :HD] / mixed[:, HD:]


def kernel(
    dims,
    fc_ref, cl_ref, sp_ref, tq_ref, cap_ref,
    out_ref,
    spv, trecv, tsend, tret, capkv, qpart, xsend, xret, acc,
    local_sem, t_s, t_r, r_s, r_r, c_s, c_r, q_s, q_r, x_s, x_r,
):
    groups, seqs, tokens, feat = dims
    heads = feat // HD
    g = lax.axis_index("group")
    s = lax.axis_index("seq")
    x, yl = s // 2, s % 2
    yh = (g // 2) % 2
    par = x % 2
    spots = tokens // seqs
    chunks = spots // ROWS_T
    cap_rows = cap_ref.shape[1]
    cap_tokens = groups * cap_rows
    partners = ((x + 1 - 2 * par) * 2 + yl, (3 - x) * 2 + yl, x * 2 + 1 - yl)
    mine = (4 * par, 4 * par + 2, 8 + 2 * yl)
    theirs = (4 - 4 * par, 6 - 4 * par, 10 - 2 * yl)

    def col(head):
        return pl.multiple_of(head * HD, HD)

    def seq_peer(i):
        return lax.rem(s + i, seqs)

    def group_peer(i):
        half = (i + 2) // 2
        offset = half + (i % 2) * (groups - 2 * half)
        peer = lax.rem(g + offset, groups)
        flip = ((peer // 2) % 2 + yh) % 2
        return peer, (yl + flip) % 2

    barrier = pltpu.get_barrier_semaphore()

    @pl.loop(1, seqs)
    def _(i):
        pl.semaphore_signal(barrier, inc=1, device_id=(g, seq_peer(i)), device_id_type=MESH)

    @pl.loop(0, groups - 1)
    def _(i):
        peer, peer_yl = group_peer(i)
        pl.semaphore_signal(barrier, inc=1, device_id=(peer, x * 2 + peer_yl), device_id_type=MESH)

    load_spatial = pltpu.make_async_copy(sp_ref.at[0, 0], spv, local_sem.at[0])
    load_spatial.start()
    pl.semaphore_wait(barrier, seqs - 1 + groups - 1)

    for i in range(SETS):
        pltpu.make_async_remote_copy(
            src_ref=sp_ref.at[0, 0, :, pl.ds(col(theirs[i]), PAIR)],
            dst_ref=qpart.at[i],
            send_sem=q_s,
            recv_sem=q_r.at[i],
            device_id=(g, partners[i]),
            device_id_type=MESH,
        ).start()

    def send_temporal(j):
        @pl.loop(1, seqs)
        def _(i):
            peer = seq_peer(i)
            pltpu.make_async_remote_copy(
                src_ref=tq_ref.at[0, 0, pl.ds(pl.multiple_of(peer * spots + j * ROWS_T, ROWS_T), ROWS_T)],
                dst_ref=trecv.at[j, s],
                send_sem=t_s,
                recv_sem=t_r.at[j],
                device_id=(g, peer),
                device_id_type=MESH,
            ).start()

    def send_captions(i):
        @pl.loop(0, groups - 1)
        def _(n):
            peer, peer_yl = group_peer(n)
            first = mine[i] if i < 2 else 8 + 2 * peer_yl
            for part in range(2):
                pltpu.make_async_remote_copy(
                    src_ref=cap_ref.at[peer, :, pl.ds(col(first + part * heads), PAIR)],
                    dst_ref=capkv.at[i, part, pl.ds(pl.multiple_of(g * cap_rows, cap_rows), cap_rows)],
                    send_sem=c_s,
                    recv_sem=c_r.at[i],
                    device_id=(peer, x * 2 + peer_yl),
                    device_id_type=MESH,
                ).start()

    for j in range(chunks):
        send_temporal(j)
        if j < SETS:
            send_captions(j)

    own = [
        pltpu.make_async_copy(
            tq_ref.at[0, 0, pl.ds(pl.multiple_of(s * spots + j * ROWS_T, ROWS_T), ROWS_T)],
            trecv.at[j, s],
            local_sem.at[1 + j],
        )
        for j in range(chunks)
    ]
    for copy in own:
        copy.start()
    own_cap = []
    for i in range(SETS):
        for part in range(2):
            copy = pltpu.make_async_copy(
                cap_ref.at[g, :, pl.ds(col(mine[i] + part * heads), PAIR)],
                capkv.at[i, part, pl.ds(pl.multiple_of(g * cap_rows, cap_rows), cap_rows)],
                local_sem.at[1 + chunks + 2 * i + part],
            )
            copy.start()
            own_cap.append(copy)

    def landed(ref, sem):
        pltpu.make_async_copy(ref, ref, sem).wait()

    frame_total = fc_ref[0]
    caption_total = cl_ref[0]

    load_spatial.wait()

    def spatial(first, count):
        @pl.loop(first, first + count)
        def _(h):
            keys_in = spv[:, pl.ds(col(heads + h), HD)]
            values = spv[:, pl.ds(col(2 * heads + h), HD)]
            for b in range(tokens // BLOCK):
                rows = pl.ds(b * BLOCK, BLOCK)
                acc[rows, pl.ds(col(h), HD)] = soft_apply(nt(spv[rows, pl.ds(col(h), HD)], keys_in), values)

    def temporal(j):
        own[j].wait()
        landed(trecv.at[j, pl.ds(0, seqs - 1)], t_r.at[j])
        size = seqs * ROWS_T
        row = lax.broadcasted_iota(jnp.int32, (size, size), 0)
        column = lax.broadcasted_iota(jnp.int32, (size, size), 1)
        keep = ((row % ROWS_T) == (column % ROWS_T)) & (column // ROWS_T < frame_total)

        @pl.loop(0, heads)
        def _(h):
            q, k, v = (
                trecv[j, :, :, pl.ds(col(part * heads + h), HD)].reshape(size, HD) for part in range(3)
            )
            mixed = soft_apply(jnp.where(keep, nt(q, k), NEG_FILL), v)
            tsend[j, :, :, pl.ds(col(h), HD)] = mixed.astype(jnp.bfloat16).reshape(seqs, ROWS_T, HD)

        home = pl.ds(pl.multiple_of(s * spots + j * ROWS_T, ROWS_T), ROWS_T)

        @pl.loop(1, seqs)
        def _(i):
            peer = seq_peer(i)
            pltpu.make_async_remote_copy(
                src_ref=tsend.at[j, peer],
                dst_ref=tret.at[home],
                send_sem=r_s,
                recv_sem=r_r,
                device_id=(g, peer),
                device_id_type=MESH,
            ).start()

        tret[home] = tsend[j, s]

    def cross(i):
        landed(qpart.at[i], q_r.at[i])
        own_cap[2 * i].wait()
        own_cap[2 * i + 1].wait()
        landed(capkv.at[i, :, pl.ds(0, cap_tokens - cap_rows)], c_r.at[i])
        token = lax.broadcasted_iota(jnp.int32, (1, cap_tokens), 1)
        bias = jnp.where(token < caption_total, 0.0, NEG_FILL)
        for k in range(2):
            lanes = pl.ds(k * HD, HD)

            @pl.loop(0, tokens // BLOCK)
            def _(b):
                rows = pl.ds(pl.multiple_of(b * BLOCK, BLOCK), BLOCK)
                scores = nt(qpart[i, rows, lanes], capkv[i, 0, :, lanes]) + bias
                xsend[i, rows, lanes] = soft_apply(scores, capkv[i, 1, :, lanes]).astype(jnp.bfloat16)

        pltpu.make_async_remote_copy(
            src_ref=xsend.at[i],
            dst_ref=xret.at[i],
            send_sem=x_s,
            recv_sem=x_r.at[i],
            device_id=(g, partners[i]),
            device_id_type=MESH,
        ).start()
        for k in range(2):
            lanes = pl.ds(k * HD, HD)
            head = pl.ds(col(mine[i] + k), HD)

            @pl.loop(0, tokens // BLOCK)
            def _(b):
                rows = pl.ds(pl.multiple_of(b * BLOCK, BLOCK), BLOCK)
                scores = nt(spv[rows, head], capkv[i, 0, :, lanes]) + bias
                acc[rows, head] += soft_apply(scores, capkv[i, 1, :, lanes])

    spatial(0, heads)
    temporal(0)
    cross(0)
    temporal(1)
    temporal(2)
    cross(1)
    temporal(3)
    cross(2)

    landed(tret.at[pl.ds(0, tokens - spots)], r_r)
    keep_frame = (s + jnp.zeros((1, 1), jnp.int32)) < frame_total

    def write(lanes, extra):
        total = acc[:, lanes] + tret[:, lanes].astype(jnp.float32)
        if extra is not None:
            total += extra
        out_ref[0, 0, :, lanes] = jnp.where(keep_frame, total, 0.0).astype(jnp.bfloat16)

    for i in range(SETS):
        write(pl.ds(col(mine[i]), PAIR), None)
    for i in range(SETS):
        landed(xret.at[i], x_r.at[i])
        write(pl.ds(col(theirs[i]), PAIR), xret[i].astype(jnp.float32))

    landed(trecv.at[:, pl.ds(0, seqs - 1)], t_s)
    landed(tsend.at[:, pl.ds(0, seqs - 1)], r_s)
    landed(capkv.at[:, :, pl.ds(0, cap_tokens - cap_rows)], c_s)
    landed(qpart, q_s)
    landed(xsend, x_s)


def body(dims, spatial_qkv, temporal_qkv, caption_kv, frame_count, caption_len):
    groups, seqs, tokens, feat = dims
    spots = tokens // seqs
    chunks = spots // ROWS_T
    cap_tokens = groups * caption_kv.shape[1]
    bf16 = jnp.bfloat16
    dma = pltpu.SemaphoreType.DMA
    return pl.pallas_call(
        functools.partial(kernel, dims),
        out_shape=jax.ShapeDtypeStruct((1, 1, tokens, feat), bf16),
        in_specs=[pl.BlockSpec(memory_space=pltpu.SMEM)] * 2 + [pl.BlockSpec(memory_space=pl.ANY)] * 3,
        out_specs=pl.BlockSpec(memory_space=pltpu.VMEM),
        scratch_shapes=[
            pltpu.VMEM((tokens, 3 * feat), bf16),
            pltpu.VMEM((chunks, seqs, ROWS_T, 3 * feat), bf16),
            pltpu.VMEM((chunks, seqs, ROWS_T, feat), bf16),
            pltpu.VMEM((tokens, feat), bf16),
            pltpu.VMEM((SETS, 2, cap_tokens, PAIR), bf16),
            pltpu.VMEM((SETS, tokens, PAIR), bf16),
            pltpu.VMEM((SETS, tokens, PAIR), bf16),
            pltpu.VMEM((SETS, tokens, PAIR), bf16),
            pltpu.VMEM((tokens, feat), jnp.float32),
            dma((1 + chunks + 2 * SETS,)),
            dma, dma((chunks,)),
            dma, dma,
            dma, dma((SETS,)),
            dma, dma((SETS,)),
            dma, dma((SETS,)),
        ],
        compiler_params=pltpu.CompilerParams(
            collective_id=0, has_side_effects=True, vmem_limit_bytes=56 << 20
        ),
    )(frame_count, caption_len, spatial_qkv, temporal_qkv, caption_kv)


def solution(mesh):
    groups, seqs = mesh.shape["group"], mesh.shape["seq"]
    placed = (
        P("group", "seq", None, None),
        P("group", "seq", None, None),
        P(None, "group", None),
        P("group"),
        P("group"),
    )

    def whole(spatial_qkv, *rest):
        dims = (groups, seqs, spatial_qkv.shape[2], spatial_qkv.shape[3] // 3)
        return jax.shard_map(
            functools.partial(body, dims),
            mesh=mesh,
            in_specs=placed,
            out_specs=P("group", "seq", None, None),
            check_vma=False,
        )(spatial_qkv, *rest)

    return whole
```

```python
import functools

import jax
import jax.numpy as jnp
from jax import lax
from jax.experimental import pallas as pl
from jax.experimental.pallas import tpu as pltpu
from jax.sharding import PartitionSpec as P

HD = 128
PAIR = 2 * HD
NEG_FILL = -1e30
LOG2E = 1.4426950408889634
MESH = pl.DeviceIdType.MESH
SETS = 3
ROWS_T = 16
UNROLL = 4


def nt(a, b):
    return lax.dot_general(a, b, (((1,), (1,)), ((), ())), preferred_element_type=jnp.float32)


def lift(scores, top):
    return jnp.exp2((scores - top) * (HD ** -0.5 * LOG2E))


def attend(queries, keys_in, values, bias=None):
    half = keys_in.shape[0] // 2
    top = None
    for part in range(2):
        span = slice(part * half, (part + 1) * half)
        scores = nt(queries, keys_in[span])
        if bias is not None:
            scores = scores + bias[:, span]
        peak = jnp.max(scores, axis=-1, keepdims=True)
        new_top = peak if top is None else jnp.maximum(top, peak)
        lifted = lift(scores, new_top)
        summed = jnp.sum(lifted, axis=-1, keepdims=True)
        mixed = jnp.dot(lifted.astype(jnp.bfloat16), values[span], preferred_element_type=jnp.float32)
        if top is not None:
            fade = lift(top, new_top)
            summed += total * fade
            mixed += out * fade
        top, total, out = new_top, summed, mixed
    return out / total


def attend_kept(queries, keys_in, values, keep):
    turned = keys_in.astype(jnp.float32).T.astype(jnp.bfloat16)
    scores = jnp.where(keep, jnp.dot(queries, turned, preferred_element_type=jnp.float32), NEG_FILL)
    lifted = lift(scores, jnp.max(scores, axis=-1, keepdims=True))
    mixed = jnp.dot(lifted.astype(jnp.bfloat16), values, preferred_element_type=jnp.float32)
    return mixed / jnp.sum(lifted, axis=-1, keepdims=True)


def kernel(
    dims,
    fc_ref, cl_ref, sp_ref, tq_ref, cap_ref,
    out_ref,
    spv, trecv, yrelay, tsend, rrelay, tret, capkv, hrelay, qpart, xsend, xret, acc,
    local_sem, y_s, y_r, t_s, f_s, t_r, a_s, b_s, b_r, g_s, r_r, h_s, h_r, c_s, d_s, c_r, q_s, q_r, x_s, x_r,
):
    groups, seqs, tokens, feat = dims
    heads = feat // HD
    xs, zs = seqs // 2, groups // 4
    g = lax.axis_index("group")
    s = lax.axis_index("seq")
    x, yl = s // 2, s % 2
    z, yh, core = g // 4, (g // 2) % 2, g % 2
    par = x % 2
    spots = tokens // seqs
    chunks = spots // ROWS_T
    cap_rows = cap_ref.shape[3]
    cap_tokens = groups * cap_rows
    y_seq = x * 2 + 1 - yl
    hi_dev = ((z * 2 + 1 - yh) * 2 + core, x * 2 + 1 - yl)
    partners = (y_seq, (x + 1 - 2 * par) * 2 + yl, (3 - x) * 2 + yl)
    mine = (8 + 2 * yl, 4 * par, 4 * par + 2)
    theirs = (10 - 2 * yl, 4 - 4 * par, 6 - 4 * par)
    hi_mine = (10 - 2 * yl, 4 * par, 4 * par + 2)

    def col(head):
        return pl.multiple_of(head * HD, HD)

    def x_peer(dx):
        return lax.rem(x + dx, xs)

    def z_peer(n):
        i = n // 2
        half = (i + 2) // 2
        offset = half + (i % 2) * (zs - 2 * half)
        last = n // (2 * zs - 2)
        return lax.rem(z + offset * (1 - last), zs), lax.rem(core + n + last, 2)

    def send(src, dst, send_sem, recv_sem, device):
        pltpu.make_async_remote_copy(
            src_ref=src, dst_ref=dst, send_sem=send_sem, recv_sem=recv_sem, device_id=device, device_id_type=MESH
        ).start()

    def landed(ref, sem):
        pltpu.make_async_copy(ref, ref, sem).wait()

    barrier = pltpu.get_barrier_semaphore()

    def greet(device):
        pl.semaphore_signal(barrier, inc=1, device_id=device, device_id_type=MESH)

    @pl.loop(1, xs)
    def _(dx):
        greet((g, x_peer(dx) * 2 + yl))

    greet((g, y_seq))
    greet(hi_dev)

    @pl.loop(0, 2 * zs - 1)
    def _(n):
        pz, pc = z_peer(n)
        greet(((pz * 2 + yh) * 2 + pc, s))

    load_spatial = pltpu.make_async_copy(sp_ref.at[0, 0], spv, local_sem.at[0])
    load_spatial.start()
    pl.semaphore_wait(barrier, xs - 1 + 2 + 2 * zs - 1)

    def spot_rows(owner, j):
        return pl.ds(pl.multiple_of(owner * spots + j * ROWS_T, ROWS_T), ROWS_T)

    def send_queries(i):
        send(sp_ref.at[0, 0, :, pl.ds(col(theirs[i]), PAIR)], qpart.at[i], q_s, q_r.at[i], (g, partners[i]))

    def send_y(j):
        @pl.loop(1, xs)
        def _(dx):
            owner = x_peer(dx) * 2 + 1 - yl
            send(tq_ref.at[0, 0, spot_rows(owner, j)], yrelay.at[j, dx - 1], y_s, y_r.at[j, dx - 1], (g, y_seq))

        send(tq_ref.at[0, 0, spot_rows(y_seq, j)], trecv.at[j, s], y_s, t_r.at[j], (g, y_seq))

    def send_x(j):
        @pl.loop(1, xs)
        def _(dx):
            owner = x_peer(dx) * 2 + yl
            send(tq_ref.at[0, 0, spot_rows(owner, j)], trecv.at[j, s], t_s, t_r.at[j], (g, owner))

    def pass_x(j):
        @pl.loop(1, xs)
        def _(dx):
            landed(yrelay.at[j, dx - 1], y_r.at[j, dx - 1])
            send(yrelay.at[j, dx - 1], trecv.at[j, y_seq], f_s, t_r.at[j], (g, x_peer(dx) * 2 + yl))

    def cap_slot(group):
        return pl.ds(pl.multiple_of(group * cap_rows, cap_rows), cap_rows)

    def send_hi(i):
        for part in range(2):
            send(
                cap_ref.at[:, 1 - yh, :, :, pl.ds(col(hi_mine[i] + part * heads), PAIR)],
                hrelay.at[i, :, :, part],
                h_s,
                h_r.at[i],
                hi_dev,
            )

    def send_z(i):
        @pl.loop(0, 2 * zs - 1)
        def _(n):
            pz, pc = z_peer(n)
            for part in range(2):
                send(
                    cap_ref.at[pz, yh, pc, :, pl.ds(col(mine[i] + part * heads), PAIR)],
                    capkv.at[i, part, cap_slot(g)],
                    c_s,
                    c_r.at[i],
                    ((pz * 2 + yh) * 2 + pc, s),
                )

    def own_z(i, part):
        return pltpu.make_async_copy(
            cap_ref.at[z, yh, core, :, pl.ds(col(mine[i] + part * heads), PAIR)],
            capkv.at[i, part, cap_slot(g)],
            local_sem.at[1 + chunks + 2 * i + part],
        )

    def own_pass(i):
        return pltpu.make_async_copy(
            hrelay.at[i, z, core], capkv.at[i, :, cap_slot(hi_dev[0])], local_sem.at[1 + chunks + 2 * SETS + i]
        )

    def pass_z(i):
        landed(hrelay.at[i], h_r.at[i])

        @pl.loop(0, 2 * zs - 1)
        def _(n):
            pz, pc = z_peer(n)
            send(
                hrelay.at[i, pz, pc],
                capkv.at[i, :, cap_slot(hi_dev[0])],
                d_s,
                c_r.at[i],
                ((pz * 2 + yh) * 2 + pc, s),
            )

        own_pass(i).start()

    def own_t(j):
        return pltpu.make_async_copy(tq_ref.at[0, 0, spot_rows(s, j)], trecv.at[j, s], local_sem.at[1 + j])

    frame_total = fc_ref[0]
    caption_total = cl_ref[0]

    def spatial(first, count):
        @pl.loop(first, first + count)
        def _(h):
            q, k, v = (spv[:, pl.ds(col(part * heads + h), HD)] for part in range(3))
            acc[:, pl.ds(col(h), HD)] = attend(q, k, v)

    def temporal(j):
        own_t(j).wait()
        landed(trecv.at[j, pl.ds(0, seqs - 1)], t_r.at[j])
        size = seqs * ROWS_T
        row = lax.broadcasted_iota(jnp.int32, (size, size), 0)
        column = lax.broadcasted_iota(jnp.int32, (size, size), 1)
        keep = ((row % ROWS_T) == (column % ROWS_T)) & (column // ROWS_T < frame_total)

        @pl.loop(0, heads // UNROLL)
        def _(n):
            for u in range(UNROLL):
                h = n * UNROLL + u
                q, k, v = (
                    trecv[j, :, :, pl.ds(col(part * heads + h), HD)].reshape(size, HD) for part in range(3)
                )
                mixed = attend_kept(q, k, v, keep)
                tsend[j, :, :, pl.ds(col(h), HD)] = mixed.astype(jnp.bfloat16).reshape(seqs, ROWS_T, HD)

        home = spot_rows(s, j)
        send(tsend.at[j, y_seq], tret.at[home], b_s, r_r, (g, y_seq))

        @pl.loop(1, xs)
        def _(dx):
            send(tsend.at[j, x_peer(dx) * 2 + 1 - yl], rrelay.at[j, dx - 1], b_s, b_r.at[j], (g, y_seq))

        @pl.loop(1, xs)
        def _(dx):
            peer = x_peer(dx) * 2 + yl
            send(tsend.at[j, peer], tret.at[home], a_s, r_r, (g, peer))

        tret[home] = tsend[j, s]

    def pass_back(j):
        landed(rrelay.at[j], b_r.at[j])

        @pl.loop(1, xs)
        def _(dx):
            send(rrelay.at[j, dx - 1], tret.at[spot_rows(y_seq, j)], g_s, r_r, (g, x_peer(dx) * 2 + yl))

    token = lax.broadcasted_iota(jnp.int32, (1, cap_tokens), 1)
    bias = jnp.where(token < caption_total, 0.0, NEG_FILL)

    def cross_theirs(i):
        landed(qpart.at[i], q_r.at[i])
        own_z(i, 0).wait()
        own_z(i, 1).wait()
        own_pass(i).wait()
        landed(capkv.at[i, :, pl.ds(0, cap_tokens - 2 * cap_rows)], c_r.at[i])
        @pl.loop(0, 2)
        def _(k):
            lanes = pl.ds(col(k), HD)
            mixed = attend(qpart[i, :, lanes], capkv[i, 0, :, lanes], capkv[i, 1, :, lanes], bias)
            xsend[i, :, lanes] = mixed.astype(jnp.bfloat16)

    def send_cross(i):
        send(xsend.at[i], xret.at[i], x_s, x_r.at[i], (g, partners[i]))

    def cross_mine(i):
        @pl.loop(0, 2)
        def _(k):
            lanes = pl.ds(col(k), HD)
            head = pl.ds(col(mine[i] + k), HD)
            acc[:, head] += attend(spv[:, head], capkv[i, 0, :, lanes], capkv[i, 1, :, lanes], bias)

    send_y(0)
    send_x(0)
    send_hi(0)
    send_z(0)
    send_queries(0)
    send_y(1)
    send_x(1)
    send_hi(1)
    send_queries(1)
    send_queries(2)
    send_z(1)
    send_y(2)
    send_y(3)
    send_hi(2)
    for j in range(chunks):
        own_t(j).start()
    for i in range(SETS):
        own_z(i, 0).start()
        own_z(i, 1).start()
    load_spatial.wait()
    spatial(0, 6)
    pass_x(0)
    send_x(2)
    pass_z(0)
    send_z(2)
    spatial(6, 6)
    pass_z(1)
    pass_x(1)
    send_x(3)
    temporal(0)
    pass_z(2)
    cross_theirs(0)
    cross_mine(0)
    pass_x(2)
    temporal(1)
    pass_x(3)
    temporal(2)
    cross_theirs(1)
    send_cross(1)
    pass_back(0)
    temporal(3)
    send_cross(0)
    cross_mine(1)
    pass_back(1)
    pass_back(2)
    cross_theirs(2)
    send_cross(2)
    pass_back(3)
    cross_mine(2)

    landed(tret.at[pl.ds(0, tokens - spots)], r_r)
    keep_frame = (s + jnp.zeros((1, 1), jnp.int32)) < frame_total

    def write(lanes, extra):
        total = acc[:, lanes] + tret[:, lanes].astype(jnp.float32)
        if extra is not None:
            total += extra
        out_ref[0, 0, :, lanes] = jnp.where(keep_frame, total, 0.0).astype(jnp.bfloat16)

    for i in range(SETS):
        write(pl.ds(col(mine[i]), PAIR), None)
    for i in range(SETS):
        landed(xret.at[i], x_r.at[i])
        write(pl.ds(col(theirs[i]), PAIR), xret[i].astype(jnp.float32))

    landed(trecv.at[:, pl.ds(0, xs)], y_s)
    landed(trecv.at[:, pl.ds(0, xs - 1)], t_s)
    landed(yrelay, f_s)
    landed(tsend.at[:, pl.ds(0, xs)], b_s)
    landed(tsend.at[:, pl.ds(0, xs - 1)], a_s)
    landed(rrelay, g_s)
    landed(capkv.at[:, :, pl.ds(0, (2 * zs - 1) * cap_rows)], c_s)
    landed(capkv.at[:, :, pl.ds(0, (2 * zs - 1) * cap_rows)], d_s)
    landed(hrelay, h_s)
    landed(qpart, q_s)
    landed(xsend, x_s)


def body(dims, spatial_qkv, temporal_qkv, caption_kv, frame_count, caption_len):
    groups, seqs, tokens, feat = dims
    spots = tokens // seqs
    chunks = spots // ROWS_T
    cap_rows = caption_kv.shape[1]
    cap_tokens = groups * cap_rows
    caption_kv = caption_kv.reshape(groups // 4, 2, 2, cap_rows, 2 * feat)
    bf16 = jnp.bfloat16
    dma = pltpu.SemaphoreType.DMA
    return pl.pallas_call(
        functools.partial(kernel, dims),
        out_shape=jax.ShapeDtypeStruct((1, 1, tokens, feat), bf16),
        in_specs=[pl.BlockSpec(memory_space=pltpu.SMEM)] * 2 + [pl.BlockSpec(memory_space=pl.ANY)] * 3,
        out_specs=pl.BlockSpec(memory_space=pltpu.VMEM),
        scratch_shapes=[
            pltpu.VMEM((tokens, 3 * feat), bf16),
            pltpu.VMEM((chunks, seqs, ROWS_T, 3 * feat), bf16),
            pltpu.VMEM((chunks, seqs // 2 - 1, ROWS_T, 3 * feat), bf16),
            pltpu.VMEM((chunks, seqs, ROWS_T, feat), bf16),
            pltpu.VMEM((chunks, seqs // 2 - 1, ROWS_T, feat), bf16),
            pltpu.VMEM((tokens, feat), bf16),
            pltpu.VMEM((SETS, 2, cap_tokens, PAIR), bf16),
            pltpu.VMEM((SETS, groups // 4, 2, 2, cap_rows, PAIR), bf16),
            pltpu.VMEM((SETS, tokens, PAIR), bf16),
            pltpu.VMEM((SETS, tokens, PAIR), bf16),
            pltpu.VMEM((SETS, tokens, PAIR), bf16),
            pltpu.VMEM((tokens, feat), jnp.float32),
            dma((1 + chunks + 3 * SETS,)),
            dma, dma((chunks, seqs // 2 - 1)),
            dma, dma, dma((chunks,)),
            dma, dma, dma((chunks,)), dma, dma,
            dma, dma((SETS,)),
            dma, dma, dma((SETS,)),
            dma, dma((SETS,)),
            dma, dma((SETS,)),
        ],
        compiler_params=pltpu.CompilerParams(
            collective_id=0, has_side_effects=True, vmem_limit_bytes=56 << 20
        ),
    )(frame_count, caption_len, spatial_qkv, temporal_qkv, caption_kv)


def solution(mesh):
    groups, seqs = mesh.shape["group"], mesh.shape["seq"]
    placed = (
        P("group", "seq", None, None),
        P("group", "seq", None, None),
        P(None, "group", None),
        P("group"),
        P("group"),
    )

    def whole(spatial_qkv, *rest):
        dims = (groups, seqs, spatial_qkv.shape[2], spatial_qkv.shape[3] // 3)
        return jax.shard_map(
            functools.partial(body, dims),
            mesh=mesh,
            in_specs=placed,
            out_specs=P("group", "seq", None, None),
            check_vma=False,
        )(spatial_qkv, *rest)

    return whole
```

```python
import functools

import jax
import jax.numpy as jnp
from jax import lax
from jax.experimental import pallas as pl
from jax.experimental.pallas import tpu as pltpu
from jax.sharding import PartitionSpec as P

HD = 128
PAIR = 2 * HD
NEG_FILL = -1e30
LOG2E = 1.4426950408889634
MESH = pl.DeviceIdType.MESH
SETS = 3
PARCELS = ((0, 0, 2), (1, 0, 2), (2, 0, 1), (2, 1, 1))
ROWS_T = 16
UNROLL = 4


def nt(a, b):
    return lax.dot_general(a, b, (((1,), (1,)), ((), ())), preferred_element_type=jnp.float32)


def lift(scores, top):
    return jnp.exp2((scores - top) * (HD ** -0.5 * LOG2E))


def attend(queries, keys_in, values, bias=None):
    half = keys_in.shape[0] // 2
    top = None
    for part in range(2):
        span = slice(part * half, (part + 1) * half)
        scores = nt(queries, keys_in[span])
        if bias is not None:
            scores = scores + bias[:, span]
        peak = jnp.max(scores, axis=-1, keepdims=True)
        new_top = peak if top is None else jnp.maximum(top, peak)
        lifted = lift(scores, new_top)
        summed = jnp.sum(lifted, axis=-1, keepdims=True)
        mixed = jnp.dot(lifted.astype(jnp.bfloat16), values[span], preferred_element_type=jnp.float32)
        if top is not None:
            fade = lift(top, new_top)
            summed += total * fade
            mixed += out * fade
        top, total, out = new_top, summed, mixed
    return out / total


def attend_kept(queries, keys_in, values, keep):
    turned = keys_in.astype(jnp.float32).T.astype(jnp.bfloat16)
    scores = jnp.where(keep, jnp.dot(queries, turned, preferred_element_type=jnp.float32), NEG_FILL)
    lifted = lift(scores, jnp.max(scores, axis=-1, keepdims=True))
    mixed = jnp.dot(lifted.astype(jnp.bfloat16), values, preferred_element_type=jnp.float32)
    return mixed / jnp.sum(lifted, axis=-1, keepdims=True)


def kernel(
    dims,
    fc_ref, cl_ref, sp_ref, tq_ref, cap_ref,
    out_ref,
    spv, trecv, yrelay, tsend, rrelay, tret, capkv, hrelay, qpart, xsend, xret, acc,
    near_sem, far_sem, local_sem, y_s, y_r, t_s, f_s, t_r, a_s, b_s, b_r, g_s, r_r, h_s, h_r, c_s, d_s, c_r, q_s, q_r, x_s, x_r,
):
    groups, seqs, tokens, feat = dims
    heads = feat // HD
    xs, zs = seqs // 2, groups // 4
    g = lax.axis_index("group")
    s = lax.axis_index("seq")
    x, yl = s // 2, s % 2
    z, yh, core = g // 4, (g // 2) % 2, g % 2
    par = x % 2
    spots = tokens // seqs
    chunks = spots // ROWS_T
    cap_rows = cap_ref.shape[3]
    cap_tokens = groups * cap_rows
    y_seq = x * 2 + 1 - yl
    hi_dev = ((z * 2 + 1 - yh) * 2 + core, x * 2 + 1 - yl)
    partners = (y_seq, (x + 1 - 2 * par) * 2 + yl, (3 - x) * 2 + yl)
    mine = (8 + 2 * yl, 4 * par, 4 * par + 2)
    theirs = (10 - 2 * yl, 4 - 4 * par, 6 - 4 * par)
    hi_mine = (10 - 2 * yl, 4 * par, 4 * par + 2)

    def col(head):
        return pl.multiple_of(head * HD, HD)

    def x_peer(dx):
        return lax.rem(x + dx, xs)

    def z_peer(n):
        i = n // 2
        half = (i + 2) // 2
        offset = half + (i % 2) * (zs - 2 * half)
        last = n // (2 * zs - 2)
        return lax.rem(z + offset * (1 - last), zs), lax.rem(core + n + last, 2)

    def send(src, dst, send_sem, recv_sem, device):
        pltpu.make_async_remote_copy(
            src_ref=src, dst_ref=dst, send_sem=send_sem, recv_sem=recv_sem, device_id=device, device_id_type=MESH
        ).start()

    def landed(ref, sem):
        pltpu.make_async_copy(ref, ref, sem).wait()

    barrier = pltpu.get_barrier_semaphore()
    first_core = g - core
    other_core = (first_core + 1 - core, s)

    def greet(device):
        pl.semaphore_signal(barrier, inc=1, device_id=device, device_id_type=MESH)

    @pl.loop(1, xs)
    def _(dx):
        greet((first_core, x_peer(dx) * 2 + yl))

    greet((first_core, y_seq))
    greet((hi_dev[0] - core, hi_dev[1]))

    @pl.loop(1, zs)
    def _(dz):
        greet(((lax.rem(z + dz, zs) * 2 + yh) * 2 + 1, s))

    @pl.when(core == 1)
    def _():
        greet(other_core)

    load_spatial = pltpu.make_async_copy(sp_ref.at[0, 0], spv, local_sem.at[0])
    load_spatial.start()

    @pl.when(core == 0)
    def _():
        pl.semaphore_wait(barrier, 2 * (xs + 1) + 1)
        pl.semaphore_signal(near_sem, inc=1, device_id=other_core, device_id_type=MESH)

    @pl.when(core == 1)
    def _():
        pl.semaphore_wait(near_sem, 1)

    def wait_far():
        @pl.when(core == 1)
        def _():
            pl.semaphore_wait(barrier, 2 * (zs - 1))
            pl.semaphore_signal(far_sem, inc=1, device_id=other_core, device_id_type=MESH)

        @pl.when(core == 0)
        def _():
            pl.semaphore_wait(far_sem, 1)

    def spot_rows(owner, j):
        return pl.ds(pl.multiple_of(owner * spots + j * ROWS_T, ROWS_T), ROWS_T)

    def send_queries(i):
        send(sp_ref.at[0, 0, :, pl.ds(col(theirs[i]), PAIR)], qpart.at[i], q_s, q_r.at[i], (g, partners[i]))

    def send_y(j):
        @pl.loop(1, xs)
        def _(dx):
            owner = x_peer(dx) * 2 + 1 - yl
            send(tq_ref.at[0, 0, spot_rows(owner, j)], yrelay.at[j, dx - 1], y_s, y_r.at[j, dx - 1], (g, y_seq))

        send(tq_ref.at[0, 0, spot_rows(y_seq, j)], trecv.at[j, s], y_s, t_r.at[j], (g, y_seq))

    def send_x(j):
        @pl.loop(1, xs)
        def _(dx):
            owner = x_peer(dx) * 2 + yl
            send(tq_ref.at[0, 0, spot_rows(owner, j)], trecv.at[j, s], t_s, t_r.at[j], (g, owner))

    def pass_x(j):
        @pl.loop(1, xs)
        def _(dx):
            landed(yrelay.at[j, dx - 1], y_r.at[j, dx - 1])
            send(yrelay.at[j, dx - 1], trecv.at[j, y_seq], f_s, t_r.at[j], (g, x_peer(dx) * 2 + yl))

    def cap_slot(group):
        return pl.ds(pl.multiple_of(group * cap_rows, cap_rows), cap_rows)

    def lanes_of(p):
        return pl.ds(PARCELS[p][1] * HD, PARCELS[p][2] * HD)

    def send_hi(p):
        i, first, count = PARCELS[p]
        for part in range(2):
            send(
                cap_ref.at[:, 1 - yh, :, :, pl.ds(col(hi_mine[i] + first + part * heads), count * HD)],
                hrelay.at[i, :, :, part, :, lanes_of(p)],
                h_s,
                h_r.at[p],
                hi_dev,
            )

    def send_z(p):
        i, first, count = PARCELS[p]

        @pl.loop(0, 2 * zs - 1)
        def _(n):
            pz, pc = z_peer(n)
            for part in range(2):
                send(
                    cap_ref.at[pz, yh, pc, :, pl.ds(col(mine[i] + first + part * heads), count * HD)],
                    capkv.at[i, part, cap_slot(g), lanes_of(p)],
                    c_s,
                    c_r.at[p],
                    ((pz * 2 + yh) * 2 + pc, s),
                )

    def own_z(i, part):
        return pltpu.make_async_copy(
            cap_ref.at[z, yh, core, :, pl.ds(col(mine[i] + part * heads), PAIR)],
            capkv.at[i, part, cap_slot(g)],
            local_sem.at[1 + chunks + 2 * i + part],
        )

    def own_pass(p):
        i = PARCELS[p][0]
        return pltpu.make_async_copy(
            hrelay.at[i, z, core, :, :, lanes_of(p)],
            capkv.at[i, :, cap_slot(hi_dev[0]), lanes_of(p)],
            local_sem.at[1 + chunks + 2 * SETS + p],
        )

    def pass_z(p):
        i = PARCELS[p][0]
        landed(hrelay.at[i, :, :, :, :, lanes_of(p)], h_r.at[p])

        @pl.loop(0, 2 * zs - 1)
        def _(n):
            pz, pc = z_peer(n)
            send(
                hrelay.at[i, pz, pc, :, :, lanes_of(p)],
                capkv.at[i, :, cap_slot(hi_dev[0]), lanes_of(p)],
                d_s,
                c_r.at[p],
                ((pz * 2 + yh) * 2 + pc, s),
            )

        own_pass(p).start()

    def own_t(j):
        return pltpu.make_async_copy(tq_ref.at[0, 0, spot_rows(s, j)], trecv.at[j, s], local_sem.at[1 + j])

    frame_total = fc_ref[0]
    caption_total = cl_ref[0]

    def spatial(first, count):
        @pl.loop(first, first + count)
        def _(h):
            q, k, v = (spv[:, pl.ds(col(part * heads + h), HD)] for part in range(3))
            acc[:, pl.ds(col(h), HD)] = attend(q, k, v)

    def temporal(j):
        own_t(j).wait()
        landed(trecv.at[j, pl.ds(0, seqs - 1)], t_r.at[j])
        size = seqs * ROWS_T
        row = lax.broadcasted_iota(jnp.int32, (size, size), 0)
        column = lax.broadcasted_iota(jnp.int32, (size, size), 1)
        keep = ((row % ROWS_T) == (column % ROWS_T)) & (column // ROWS_T < frame_total)

        @pl.loop(0, heads // UNROLL)
        def _(n):
            for u in range(UNROLL):
                h = n * UNROLL + u
                q, k, v = (
                    trecv[j, :, :, pl.ds(col(part * heads + h), HD)].reshape(size, HD) for part in range(3)
                )
                mixed = attend_kept(q, k, v, keep)
                tsend[j, :, :, pl.ds(col(h), HD)] = mixed.astype(jnp.bfloat16).reshape(seqs, ROWS_T, HD)

        home = spot_rows(s, j)

        @pl.loop(1, xs)
        def _(dx):
            send(tsend.at[j, x_peer(dx) * 2 + 1 - yl], rrelay.at[j, dx - 1], b_s, b_r.at[j, dx - 1], (g, y_seq))

        send(tsend.at[j, y_seq], tret.at[home], b_s, r_r, (g, y_seq))

        @pl.loop(1, xs)
        def _(dx):
            peer = x_peer(dx) * 2 + yl
            send(tsend.at[j, peer], tret.at[home], a_s, r_r, (g, peer))

        tret[home] = tsend[j, s]

    def pass_back(j):
        @pl.loop(1, xs)
        def _(dx):
            landed(rrelay.at[j, dx - 1], b_r.at[j, dx - 1])
            send(rrelay.at[j, dx - 1], tret.at[spot_rows(y_seq, j)], g_s, r_r, (g, x_peer(dx) * 2 + yl))

    token = lax.broadcasted_iota(jnp.int32, (1, cap_tokens), 1)
    bias = jnp.where(token < caption_total, 0.0, NEG_FILL)

    def cross_theirs(p):
        i, first, count = PARCELS[p]
        if first == 0:
            landed(qpart.at[i], q_r.at[i])
            own_z(i, 0).wait()
            own_z(i, 1).wait()
        own_pass(p).wait()
        landed(capkv.at[i, :, pl.ds(0, cap_tokens - 2 * cap_rows), lanes_of(p)], c_r.at[p])

        @pl.loop(first, first + count)
        def _(k):
            lanes = pl.ds(col(k), HD)
            mixed = attend(qpart[i, :, lanes], capkv[i, 0, :, lanes], capkv[i, 1, :, lanes], bias)
            xsend[i, :, lanes] = mixed.astype(jnp.bfloat16)

    def send_cross(p):
        i = PARCELS[p][0]
        send(xsend.at[i, :, lanes_of(p)], xret.at[i, :, lanes_of(p)], x_s, x_r.at[p], (g, partners[i]))

    def cross_mine(p):
        i, first, count = PARCELS[p]

        @pl.loop(first, first + count)
        def _(k):
            lanes = pl.ds(col(k), HD)
            head = pl.ds(col(mine[i] + k), HD)
            acc[:, head] += attend(spv[:, head], capkv[i, 0, :, lanes], capkv[i, 1, :, lanes], bias)

    send_y(0)
    send_x(0)
    send_hi(0)
    send_queries(0)
    send_y(1)
    send_x(1)
    send_hi(1)
    send_queries(1)
    send_queries(2)
    send_y(2)
    send_y(3)
    send_hi(2)
    send_hi(3)
    for j in range(chunks):
        own_t(j).start()
    for i in range(SETS):
        own_z(i, 0).start()
        own_z(i, 1).start()
    wait_far()
    send_z(0)
    send_z(1)
    load_spatial.wait()
    spatial(0, 4)
    pass_x(0)
    send_x(2)
    pass_z(0)
    send_z(2)
    spatial(4, 4)
    pass_z(1)
    pass_x(1)
    send_x(3)
    send_z(3)
    spatial(8, 4)
    temporal(0)
    pass_z(2)
    pass_x(2)
    cross_theirs(0)
    cross_mine(0)
    temporal(1)
    pass_z(3)
    pass_x(3)
    temporal(2)
    cross_theirs(1)
    send_cross(1)
    pass_back(0)
    temporal(3)
    send_cross(0)
    cross_mine(1)
    pass_back(1)
    pass_back(2)
    cross_theirs(2)
    send_cross(2)
    cross_mine(2)
    pass_back(3)
    cross_theirs(3)
    send_cross(3)
    cross_mine(3)

    landed(tret.at[pl.ds(0, tokens - spots)], r_r)
    keep_frame = (s + jnp.zeros((1, 1), jnp.int32)) < frame_total

    def write(lanes, extra):
        total = acc[:, lanes] + tret[:, lanes].astype(jnp.float32)
        if extra is not None:
            total += extra
        out_ref[0, 0, :, lanes] = jnp.where(keep_frame, total, 0.0).astype(jnp.bfloat16)

    for i in range(SETS):
        write(pl.ds(col(mine[i]), PAIR), None)
    for p, (i, first, count) in enumerate(PARCELS):
        landed(xret.at[i, :, lanes_of(p)], x_r.at[p])
        write(pl.ds(col(theirs[i] + first), count * HD), xret[i, :, lanes_of(p)].astype(jnp.float32))

    landed(trecv.at[:, pl.ds(0, xs)], y_s)
    landed(trecv.at[:, pl.ds(0, xs - 1)], t_s)
    landed(yrelay, f_s)
    landed(tsend.at[:, pl.ds(0, xs)], b_s)
    landed(tsend.at[:, pl.ds(0, xs - 1)], a_s)
    landed(rrelay, g_s)
    landed(capkv.at[:, :, pl.ds(0, (2 * zs - 1) * cap_rows)], c_s)
    landed(capkv.at[:, :, pl.ds(0, (2 * zs - 1) * cap_rows)], d_s)
    landed(hrelay, h_s)
    landed(qpart, q_s)
    landed(xsend, x_s)


def body(dims, spatial_qkv, temporal_qkv, caption_kv, frame_count, caption_len):
    groups, seqs, tokens, feat = dims
    spots = tokens // seqs
    chunks = spots // ROWS_T
    cap_rows = caption_kv.shape[1]
    cap_tokens = groups * cap_rows
    caption_kv = caption_kv.reshape(groups // 4, 2, 2, cap_rows, 2 * feat)
    bf16 = jnp.bfloat16
    dma = pltpu.SemaphoreType.DMA
    return pl.pallas_call(
        functools.partial(kernel, dims),
        out_shape=pltpu.VMEM((1, 1, tokens, feat), bf16),
        in_specs=[pl.BlockSpec(memory_space=pltpu.SMEM)] * 2 + [pl.BlockSpec(memory_space=pl.ANY)] * 3,
        out_specs=pl.BlockSpec(memory_space=pltpu.VMEM),
        scratch_shapes=[
            pltpu.VMEM((tokens, 3 * feat), bf16),
            pltpu.VMEM((chunks, seqs, ROWS_T, 3 * feat), bf16),
            pltpu.VMEM((chunks, seqs // 2 - 1, ROWS_T, 3 * feat), bf16),
            pltpu.VMEM((chunks, seqs, ROWS_T, feat), bf16),
            pltpu.VMEM((chunks, seqs // 2 - 1, ROWS_T, feat), bf16),
            pltpu.VMEM((tokens, feat), bf16),
            pltpu.VMEM((SETS, 2, cap_tokens, PAIR), bf16),
            pltpu.VMEM((SETS, groups // 4, 2, 2, cap_rows, PAIR), bf16),
            pltpu.VMEM((SETS, tokens, PAIR), bf16),
            pltpu.VMEM((SETS, tokens, PAIR), bf16),
            pltpu.VMEM((SETS, tokens, PAIR), bf16),
            pltpu.VMEM((tokens, feat), jnp.float32),
            pltpu.SemaphoreType.REGULAR,
            pltpu.SemaphoreType.REGULAR,
            dma((1 + chunks + 2 * SETS + len(PARCELS),)),
            dma, dma((chunks, seqs // 2 - 1)),
            dma, dma, dma((chunks,)),
            dma, dma, dma((chunks, seqs // 2 - 1)), dma, dma,
            dma, dma((len(PARCELS),)),
            dma, dma, dma((len(PARCELS),)),
            dma, dma((SETS,)),
            dma, dma((len(PARCELS),)),
        ],
        compiler_params=pltpu.CompilerParams(
            collective_id=0, has_side_effects=True, vmem_limit_bytes=56 << 20
        ),
    )(frame_count, caption_len, spatial_qkv, temporal_qkv, caption_kv)


def solution(mesh):
    groups, seqs = mesh.shape["group"], mesh.shape["seq"]
    placed = (
        P("group", "seq", None, None),
        P("group", "seq", None, None),
        P(None, "group", None),
        P("group"),
        P("group"),
    )

    def whole(spatial_qkv, *rest):
        dims = (groups, seqs, spatial_qkv.shape[2], spatial_qkv.shape[3] // 3)
        return jax.shard_map(
            functools.partial(body, dims),
            mesh=mesh,
            in_specs=placed,
            out_specs=P("group", "seq", None, None),
            check_vma=False,
        )(spatial_qkv, *rest)

    return whole
```

```python
import functools

import jax
import jax.numpy as jnp
from jax import lax
from jax.experimental import pallas as pl
from jax.experimental.pallas import tpu as pltpu
from jax.sharding import PartitionSpec as P

HD = 128
PAIR = 2 * HD
NEG_FILL = -1e30
LOG2E = 1.4426950408889634
MESH = pl.DeviceIdType.MESH
SETS = 3
PARCELS = ((0, 0, 2), (1, 0, 2), (2, 0, 1), (2, 1, 1))
ROWS_T = 16
UNROLL = 4


def nt(a, b):
    return lax.dot_general(a, b, (((1,), (1,)), ((), ())), preferred_element_type=jnp.float32)


def lift(scores, top):
    return jnp.exp2((scores - top) * (HD ** -0.5 * LOG2E))


def attend(queries, keys_in, values, bias=None):
    half = keys_in.shape[0] // 2
    top = None
    for part in range(2):
        span = slice(part * half, (part + 1) * half)
        scores = nt(queries, keys_in[span])
        if bias is not None:
            scores = scores + bias[:, span]
        peak = jnp.max(scores, axis=-1, keepdims=True)
        new_top = peak if top is None else jnp.maximum(top, peak)
        lifted = lift(scores, new_top)
        summed = jnp.sum(lifted, axis=-1, keepdims=True)
        mixed = jnp.dot(lifted.astype(jnp.bfloat16), values[span], preferred_element_type=jnp.float32)
        if top is not None:
            fade = lift(top, new_top)
            summed += total * fade
            mixed += out * fade
        top, total, out = new_top, summed, mixed
    return out / total


def attend_kept(queries, keys_in, values, keep):
    turned = keys_in.astype(jnp.float32).T.astype(jnp.bfloat16)
    scores = jnp.where(keep, jnp.dot(queries, turned, preferred_element_type=jnp.float32), NEG_FILL)
    lifted = lift(scores, jnp.max(scores, axis=-1, keepdims=True))
    mixed = jnp.dot(lifted.astype(jnp.bfloat16), values, preferred_element_type=jnp.float32)
    return mixed / jnp.sum(lifted, axis=-1, keepdims=True)


def kernel(
    dims,
    fc_ref, cl_ref, sp_ref, tq_ref, cap_ref,
    out_ref,
    spv, trecv, yrelay, tsend, rrelay, tret, capkv, hrelay, qpart, xsend, xret, acc,
    near_sem, far_sem, local_sem, y_s, y_r, t_s, f_s, t_r, a_s, b_s, b_r, g_s, r_r, h_s, h_r, c_s, d_s, c_r, q_s, q_r, x_s, x_r,
):
    groups, seqs, tokens, feat = dims
    heads = feat // HD
    xs, zs = seqs // 2, groups // 4
    g = lax.axis_index("group")
    s = lax.axis_index("seq")
    x, yl = s // 2, s % 2
    z, yh, core = g // 4, (g // 2) % 2, g % 2
    par = x % 2
    spots = tokens // seqs
    chunks = spots // ROWS_T
    cap_rows = cap_ref.shape[3]
    cap_tokens = groups * cap_rows
    y_seq = x * 2 + 1 - yl
    hi_dev = ((z * 2 + 1 - yh) * 2 + core, x * 2 + 1 - yl)
    partners = ((x + 1 - 2 * par) * 2 + yl, (3 - x) * 2 + yl, y_seq)
    mine = (4 * par, 4 * par + 2, 8 + 2 * yl)
    theirs = (4 - 4 * par, 6 - 4 * par, 10 - 2 * yl)
    hi_mine = (4 * par, 4 * par + 2, 10 - 2 * yl)

    def col(head):
        return pl.multiple_of(head * HD, HD)

    def x_peer(dx):
        return lax.rem(x + dx, xs)

    def z_peer(n):
        i = n // 2
        half = (i + 2) // 2
        offset = half + (i % 2) * (zs - 2 * half)
        last = n // (2 * zs - 2)
        return lax.rem(z + offset * (1 - last), zs), lax.rem(core + n + last, 2)

    def send(src, dst, send_sem, recv_sem, device):
        pltpu.make_async_remote_copy(
            src_ref=src, dst_ref=dst, send_sem=send_sem, recv_sem=recv_sem, device_id=device, device_id_type=MESH
        ).start()

    def landed(ref, sem):
        pltpu.make_async_copy(ref, ref, sem).wait()

    barrier = pltpu.get_barrier_semaphore()
    first_core = g - core
    other_core = (first_core + 1 - core, s)

    def greet(device):
        pl.semaphore_signal(barrier, inc=1, device_id=device, device_id_type=MESH)

    @pl.loop(1, xs)
    def _(dx):
        greet((first_core, x_peer(dx) * 2 + yl))

    greet((first_core, y_seq))
    greet((hi_dev[0] - core, hi_dev[1]))

    @pl.loop(1, zs)
    def _(dz):
        greet(((lax.rem(z + dz, zs) * 2 + yh) * 2 + 1, s))

    @pl.when(core == 1)
    def _():
        greet(other_core)

    load_spatial = pltpu.make_async_copy(sp_ref.at[0, 0], spv, local_sem.at[0])
    load_spatial.start()

    @pl.when(core == 0)
    def _():
        pl.semaphore_wait(barrier, 2 * (xs + 1) + 1)
        pl.semaphore_signal(near_sem, inc=1, device_id=other_core, device_id_type=MESH)

    @pl.when(core == 1)
    def _():
        pl.semaphore_wait(near_sem, 1)

    def wait_far():
        @pl.when(core == 1)
        def _():
            pl.semaphore_wait(barrier, 2 * (zs - 1))
            pl.semaphore_signal(far_sem, inc=1, device_id=other_core, device_id_type=MESH)

        @pl.when(core == 0)
        def _():
            pl.semaphore_wait(far_sem, 1)

    def spot_rows(owner, j):
        return pl.ds(pl.multiple_of(owner * spots + j * ROWS_T, ROWS_T), ROWS_T)

    def send_queries(i):
        send(sp_ref.at[0, 0, :, pl.ds(col(theirs[i]), PAIR)], qpart.at[i], q_s, q_r.at[i], (g, partners[i]))

    def send_y(j):
        @pl.loop(1, xs)
        def _(dx):
            owner = x_peer(dx) * 2 + 1 - yl
            send(tq_ref.at[0, 0, spot_rows(owner, j)], yrelay.at[j, dx - 1], y_s, y_r.at[j, dx - 1], (g, y_seq))

        send(tq_ref.at[0, 0, spot_rows(y_seq, j)], trecv.at[j, s], y_s, t_r.at[j], (g, y_seq))

    def send_x(j):
        @pl.loop(1, xs)
        def _(dx):
            owner = x_peer(dx) * 2 + yl
            send(tq_ref.at[0, 0, spot_rows(owner, j)], trecv.at[j, s], t_s, t_r.at[j], (g, owner))

    def pass_x(j):
        @pl.loop(1, xs)
        def _(dx):
            landed(yrelay.at[j, dx - 1], y_r.at[j, dx - 1])
            send(yrelay.at[j, dx - 1], trecv.at[j, y_seq], f_s, t_r.at[j], (g, x_peer(dx) * 2 + yl))

    def cap_slot(group):
        return pl.ds(pl.multiple_of(group * cap_rows, cap_rows), cap_rows)

    def lanes_of(p):
        return pl.ds(PARCELS[p][1] * HD, PARCELS[p][2] * HD)

    def send_hi(p):
        i, first, count = PARCELS[p]
        for part in range(2):
            send(
                cap_ref.at[:, 1 - yh, :, :, pl.ds(col(hi_mine[i] + first + part * heads), count * HD)],
                hrelay.at[i, :, :, part, :, lanes_of(p)],
                h_s,
                h_r.at[p],
                hi_dev,
            )

    def send_z(p):
        i, first, count = PARCELS[p]

        @pl.loop(0, 2 * zs - 1)
        def _(n):
            pz, pc = z_peer(n)
            for part in range(2):
                send(
                    cap_ref.at[pz, yh, pc, :, pl.ds(col(mine[i] + first + part * heads), count * HD)],
                    capkv.at[i, part, cap_slot(g), lanes_of(p)],
                    c_s,
                    c_r.at[p],
                    ((pz * 2 + yh) * 2 + pc, s),
                )

    def own_z(i, part):
        return pltpu.make_async_copy(
            cap_ref.at[z, yh, core, :, pl.ds(col(mine[i] + part * heads), PAIR)],
            capkv.at[i, part, cap_slot(g)],
            local_sem.at[1 + chunks + 2 * i + part],
        )

    def own_pass(p):
        i = PARCELS[p][0]
        return pltpu.make_async_copy(
            hrelay.at[i, z, core, :, :, lanes_of(p)],
            capkv.at[i, :, cap_slot(hi_dev[0]), lanes_of(p)],
            local_sem.at[1 + chunks + 2 * SETS + p],
        )

    def pass_z(p):
        i = PARCELS[p][0]
        landed(hrelay.at[i, :, :, :, :, lanes_of(p)], h_r.at[p])

        @pl.loop(0, 2 * zs - 1)
        def _(n):
            pz, pc = z_peer(n)
            send(
                hrelay.at[i, pz, pc, :, :, lanes_of(p)],
                capkv.at[i, :, cap_slot(hi_dev[0]), lanes_of(p)],
                d_s,
                c_r.at[p],
                ((pz * 2 + yh) * 2 + pc, s),
            )

        own_pass(p).start()

    def own_t(j):
        return pltpu.make_async_copy(tq_ref.at[0, 0, spot_rows(s, j)], trecv.at[j, s], local_sem.at[1 + j])

    frame_total = fc_ref[0]
    caption_total = cl_ref[0]

    def spatial(first, count):
        @pl.loop(first, first + count)
        def _(h):
            q, k, v = (spv[:, pl.ds(col(part * heads + h), HD)] for part in range(3))
            acc[:, pl.ds(col(h), HD)] = attend(q, k, v)

    def temporal(j):
        own_t(j).wait()
        landed(trecv.at[j, pl.ds(0, seqs - 1)], t_r.at[j])
        size = seqs * ROWS_T
        row = lax.broadcasted_iota(jnp.int32, (size, size), 0)
        column = lax.broadcasted_iota(jnp.int32, (size, size), 1)
        keep = ((row % ROWS_T) == (column % ROWS_T)) & (column // ROWS_T < frame_total)

        @pl.loop(0, heads // UNROLL)
        def _(n):
            for u in range(UNROLL):
                h = n * UNROLL + u
                q, k, v = (
                    trecv[j, :, :, pl.ds(col(part * heads + h), HD)].reshape(size, HD) for part in range(3)
                )
                mixed = attend_kept(q, k, v, keep)
                tsend[j, :, :, pl.ds(col(h), HD)] = mixed.astype(jnp.bfloat16).reshape(seqs, ROWS_T, HD)

        home = spot_rows(s, j)

        @pl.loop(1, xs)
        def _(dx):
            send(tsend.at[j, x_peer(dx) * 2 + 1 - yl], rrelay.at[j, dx - 1], b_s, b_r.at[j, dx - 1], (g, y_seq))

        send(tsend.at[j, y_seq], tret.at[home], b_s, r_r, (g, y_seq))

        @pl.loop(1, xs)
        def _(dx):
            peer = x_peer(dx) * 2 + yl
            send(tsend.at[j, peer], tret.at[home], a_s, r_r, (g, peer))

        tret[home] = tsend[j, s]

    def pass_back(j):
        @pl.loop(1, xs)
        def _(dx):
            landed(rrelay.at[j, dx - 1], b_r.at[j, dx - 1])
            send(rrelay.at[j, dx - 1], tret.at[spot_rows(y_seq, j)], g_s, r_r, (g, x_peer(dx) * 2 + yl))

    token = lax.broadcasted_iota(jnp.int32, (1, cap_tokens), 1)
    bias = jnp.where(token < caption_total, 0.0, NEG_FILL)

    def cross_theirs(p):
        i, first, count = PARCELS[p]
        if first == 0:
            landed(qpart.at[i], q_r.at[i])
            own_z(i, 0).wait()
            own_z(i, 1).wait()
        own_pass(p).wait()
        landed(capkv.at[i, :, pl.ds(0, cap_tokens - 2 * cap_rows), lanes_of(p)], c_r.at[p])

        @pl.loop(first, first + count)
        def _(k):
            lanes = pl.ds(col(k), HD)
            mixed = attend(qpart[i, :, lanes], capkv[i, 0, :, lanes], capkv[i, 1, :, lanes], bias)
            xsend[i, :, lanes] = mixed.astype(jnp.bfloat16)

    def send_cross(p):
        i = PARCELS[p][0]
        send(xsend.at[i, :, lanes_of(p)], xret.at[i, :, lanes_of(p)], x_s, x_r.at[p], (g, partners[i]))

    def cross_mine(p):
        i, first, count = PARCELS[p]

        @pl.loop(first, first + count)
        def _(k):
            lanes = pl.ds(col(k), HD)
            head = pl.ds(col(mine[i] + k), HD)
            acc[:, head] += attend(spv[:, head], capkv[i, 0, :, lanes], capkv[i, 1, :, lanes], bias)

    send_y(0)
    send_x(0)
    send_hi(0)
    send_y(1)
    send_x(1)
    send_hi(1)
    send_queries(0)
    send_queries(1)
    send_y(2)
    send_y(3)
    send_queries(2)
    send_hi(2)
    send_hi(3)
    for j in range(chunks):
        own_t(j).start()
    for i in range(SETS):
        own_z(i, 0).start()
        own_z(i, 1).start()
    wait_far()
    send_z(0)
    send_z(1)
    load_spatial.wait()
    spatial(0, 4)
    pass_x(0)
    send_x(2)
    pass_z(0)
    send_z(2)
    spatial(4, 4)
    pass_z(1)
    pass_x(1)
    send_x(3)
    send_z(3)
    temporal(0)
    pass_z(2)
    spatial(8, 2)
    pass_x(2)
    temporal(1)
    cross_theirs(0)
    pass_z(3)
    spatial(10, 2)
    pass_x(3)
    send_cross(0)
    temporal(2)
    cross_theirs(1)
    send_cross(1)
    pass_back(0)
    temporal(3)
    cross_mine(0)
    pass_back(1)
    cross_mine(1)
    pass_back(2)
    cross_theirs(2)
    send_cross(2)
    pass_back(3)
    cross_theirs(3)
    send_cross(3)
    cross_mine(2)
    cross_mine(3)

    landed(tret.at[pl.ds(0, tokens - spots)], r_r)
    keep_frame = (s + jnp.zeros((1, 1), jnp.int32)) < frame_total

    def write(lanes, extra):
        total = acc[:, lanes] + tret[:, lanes].astype(jnp.float32)
        if extra is not None:
            total += extra
        out_ref[0, 0, :, lanes] = jnp.where(keep_frame, total, 0.0).astype(jnp.bfloat16)

    for i in range(SETS):
        write(pl.ds(col(mine[i]), PAIR), None)
    for p, (i, first, count) in enumerate(PARCELS):
        landed(xret.at[i, :, lanes_of(p)], x_r.at[p])
        write(pl.ds(col(theirs[i] + first), count * HD), xret[i, :, lanes_of(p)].astype(jnp.float32))

    landed(trecv.at[:, pl.ds(0, xs)], y_s)
    landed(trecv.at[:, pl.ds(0, xs - 1)], t_s)
    landed(yrelay, f_s)
    landed(tsend.at[:, pl.ds(0, xs)], b_s)
    landed(tsend.at[:, pl.ds(0, xs - 1)], a_s)
    landed(rrelay, g_s)
    landed(capkv.at[:, :, pl.ds(0, (2 * zs - 1) * cap_rows)], c_s)
    landed(capkv.at[:, :, pl.ds(0, (2 * zs - 1) * cap_rows)], d_s)
    landed(hrelay, h_s)
    landed(qpart, q_s)
    landed(xsend, x_s)


def body(dims, spatial_qkv, temporal_qkv, caption_kv, frame_count, caption_len):
    groups, seqs, tokens, feat = dims
    spots = tokens // seqs
    chunks = spots // ROWS_T
    cap_rows = caption_kv.shape[1]
    cap_tokens = groups * cap_rows
    caption_kv = caption_kv.reshape(groups // 4, 2, 2, cap_rows, 2 * feat)
    bf16 = jnp.bfloat16
    dma = pltpu.SemaphoreType.DMA
    return pl.pallas_call(
        functools.partial(kernel, dims),
        out_shape=pltpu.VMEM((1, 1, tokens, feat), bf16),
        in_specs=[pl.BlockSpec(memory_space=pltpu.SMEM)] * 2 + [pl.BlockSpec(memory_space=pl.ANY)] * 3,
        out_specs=pl.BlockSpec(memory_space=pltpu.VMEM),
        scratch_shapes=[
            pltpu.VMEM((tokens, 3 * feat), bf16),
            pltpu.VMEM((chunks, seqs, ROWS_T, 3 * feat), bf16),
            pltpu.VMEM((chunks, seqs // 2 - 1, ROWS_T, 3 * feat), bf16),
            pltpu.VMEM((chunks, seqs, ROWS_T, feat), bf16),
            pltpu.VMEM((chunks, seqs // 2 - 1, ROWS_T, feat), bf16),
            pltpu.VMEM((tokens, feat), bf16),
            pltpu.VMEM((SETS, 2, cap_tokens, PAIR), bf16),
            pltpu.VMEM((SETS, groups // 4, 2, 2, cap_rows, PAIR), bf16),
            pltpu.VMEM((SETS, tokens, PAIR), bf16),
            pltpu.VMEM((SETS, tokens, PAIR), bf16),
            pltpu.VMEM((SETS, tokens, PAIR), bf16),
            pltpu.VMEM((tokens, feat), jnp.float32),
            pltpu.SemaphoreType.REGULAR,
            pltpu.SemaphoreType.REGULAR,
            dma((1 + chunks + 2 * SETS + len(PARCELS),)),
            dma, dma((chunks, seqs // 2 - 1)),
            dma, dma, dma((chunks,)),
            dma, dma, dma((chunks, seqs // 2 - 1)), dma, dma,
            dma, dma((len(PARCELS),)),
            dma, dma, dma((len(PARCELS),)),
            dma, dma((SETS,)),
            dma, dma((len(PARCELS),)),
        ],
        compiler_params=pltpu.CompilerParams(
            collective_id=0, has_side_effects=True, vmem_limit_bytes=56 << 20
        ),
    )(frame_count, caption_len, spatial_qkv, temporal_qkv, caption_kv)


def solution(mesh):
    groups, seqs = mesh.shape["group"], mesh.shape["seq"]
    placed = (
        P("group", "seq", None, None),
        P("group", "seq", None, None),
        P(None, "group", None),
        P("group"),
        P("group"),
    )

    def whole(spatial_qkv, *rest):
        dims = (groups, seqs, spatial_qkv.shape[2], spatial_qkv.shape[3] // 3)
        return jax.shard_map(
            functools.partial(body, dims),
            mesh=mesh,
            in_specs=placed,
            out_specs=P("group", "seq", None, None),
            check_vma=False,
        )(spatial_qkv, *rest)

    return whole
```

```python
import functools

import jax
import jax.numpy as jnp
from jax import lax
from jax.experimental import pallas as pl
from jax.experimental.pallas import tpu as pltpu
from jax.sharding import PartitionSpec as P

HD = 128
PAIR = 2 * HD
NEG_FILL = -1e30
LOG2E = 1.4426950408889634
MESH = pl.DeviceIdType.MESH
SETS = 3
PARCELS = ((0, 0, 2), (1, 0, 2), (2, 0, 1), (2, 1, 1))
ROWS_T = 16
UNROLL = 4


def nt(a, b):
    return lax.dot_general(a, b, (((1,), (1,)), ((), ())), preferred_element_type=jnp.float32)


def lift(scores, top):
    return jnp.exp2((scores - top) * (HD ** -0.5 * LOG2E))


def attend(queries, keys_in, values, bias=None):
    half = keys_in.shape[0] // 2
    top = None
    for part in range(2):
        span = slice(part * half, (part + 1) * half)
        scores = nt(queries, keys_in[span])
        if bias is not None:
            scores = scores + bias[:, span]
        peak = jnp.max(scores, axis=-1, keepdims=True)
        new_top = peak if top is None else jnp.maximum(top, peak)
        lifted = lift(scores, new_top)
        summed = jnp.sum(lifted, axis=-1, keepdims=True)
        mixed = jnp.dot(lifted.astype(jnp.bfloat16), values[span], preferred_element_type=jnp.float32)
        if top is not None:
            fade = lift(top, new_top)
            summed += total * fade
            mixed += out * fade
        top, total, out = new_top, summed, mixed
    return out / total


def attend_kept(queries, keys_in, values, keep):
    turned = keys_in.astype(jnp.float32).T.astype(jnp.bfloat16)
    scores = jnp.where(keep, jnp.dot(queries, turned, preferred_element_type=jnp.float32), NEG_FILL)
    lifted = lift(scores, jnp.max(scores, axis=-1, keepdims=True))
    mixed = jnp.dot(lifted.astype(jnp.bfloat16), values, preferred_element_type=jnp.float32)
    return mixed / jnp.sum(lifted, axis=-1, keepdims=True)


def kernel(
    dims,
    fc_hbm, cl_hbm, sp_ref, tq_ref, cap_ref,
    out_ref,
    spv, trecv, yrelay, tsend, rrelay, tret, capkv, hrelay, qpart, xsend, xret, acc,
    fc_ref, cl_ref, near_sem, far_sem, scalar_sem, local_sem, y_s, y_r, t_s, f_s, t_r, a_s, b_s, b_r, g_s, r_r, h_s, h_r, c_s, d_s, c_r, q_s, q_r, x_s, x_r,
):
    groups, seqs, tokens, feat = dims
    heads = feat // HD
    xs, zs = seqs // 2, groups // 4
    g = lax.axis_index("group")
    s = lax.axis_index("seq")
    x, yl = s // 2, s % 2
    z, yh, core = g // 4, (g // 2) % 2, g % 2
    par = x % 2
    spots = tokens // seqs
    chunks = spots // ROWS_T
    cap_rows = cap_ref.shape[3]
    cap_tokens = groups * cap_rows
    y_seq = x * 2 + 1 - yl
    hi_dev = ((z * 2 + 1 - yh) * 2 + core, x * 2 + 1 - yl)
    partners = ((x + 1 - 2 * par) * 2 + yl, (3 - x) * 2 + yl, y_seq)
    mine = (4 * par, 4 * par + 2, 8 + 2 * yl)
    theirs = (4 - 4 * par, 6 - 4 * par, 10 - 2 * yl)
    hi_mine = (4 * par, 4 * par + 2, 10 - 2 * yl)

    def col(head):
        return pl.multiple_of(head * HD, HD)

    def x_peer(dx):
        return lax.rem(x + dx, xs)

    def z_peer(n):
        i = n // 2
        half = (i + 2) // 2
        offset = half + (i % 2) * (zs - 2 * half)
        last = n // (2 * zs - 2)
        return lax.rem(z + offset * (1 - last), zs), lax.rem(core + n + last, 2)

    def send(src, dst, send_sem, recv_sem, device):
        pltpu.make_async_remote_copy(
            src_ref=src, dst_ref=dst, send_sem=send_sem, recv_sem=recv_sem, device_id=device, device_id_type=MESH
        ).start()

    def landed(ref, sem):
        pltpu.make_async_copy(ref, ref, sem).wait()

    barrier = pltpu.get_barrier_semaphore()
    first_core = g - core
    other_core = (first_core + 1 - core, s)

    def greet(device):
        pl.semaphore_signal(barrier, inc=1, device_id=device, device_id_type=MESH)

    @pl.loop(1, xs)
    def _(dx):
        greet((first_core, x_peer(dx) * 2 + yl))

    greet((first_core, y_seq))
    greet((hi_dev[0] - core, hi_dev[1]))

    @pl.loop(1, zs)
    def _(dz):
        greet(((lax.rem(z + dz, zs) * 2 + yh) * 2 + 1, s))

    @pl.when(core == 1)
    def _():
        greet(other_core)

    load_spatial = pltpu.make_async_copy(sp_ref.at[0, 0], spv, local_sem.at[0])
    load_spatial.start()
    counts = [
        pltpu.make_async_copy(fc_hbm, fc_ref, scalar_sem.at[0]),
        pltpu.make_async_copy(cl_hbm, cl_ref, scalar_sem.at[1]),
    ]
    for copy in counts:
        copy.start()

    @pl.when(core == 0)
    def _():
        pl.semaphore_wait(barrier, 2 * (xs + 1) + 1)
        pl.semaphore_signal(near_sem, inc=1, device_id=other_core, device_id_type=MESH)

    @pl.when(core == 1)
    def _():
        pl.semaphore_wait(near_sem, 1)

    def wait_far():
        @pl.when(core == 1)
        def _():
            pl.semaphore_wait(barrier, 2 * (zs - 1))
            pl.semaphore_signal(far_sem, inc=1, device_id=other_core, device_id_type=MESH)

        @pl.when(core == 0)
        def _():
            pl.semaphore_wait(far_sem, 1)

    def spot_rows(owner, j):
        return pl.ds(pl.multiple_of(owner * spots + j * ROWS_T, ROWS_T), ROWS_T)

    def send_queries(i):
        send(sp_ref.at[0, 0, :, pl.ds(col(theirs[i]), PAIR)], qpart.at[i], q_s, q_r.at[i], (g, partners[i]))

    def send_y(j):
        @pl.loop(1, xs)
        def _(dx):
            owner = x_peer(dx) * 2 + 1 - yl
            send(tq_ref.at[0, 0, spot_rows(owner, j)], yrelay.at[j, dx - 1], y_s, y_r.at[j, dx - 1], (g, y_seq))

        send(tq_ref.at[0, 0, spot_rows(y_seq, j)], trecv.at[j, s], y_s, t_r.at[j], (g, y_seq))

    def send_x(j):
        @pl.loop(1, xs)
        def _(dx):
            owner = x_peer(dx) * 2 + yl
            send(tq_ref.at[0, 0, spot_rows(owner, j)], trecv.at[j, s], t_s, t_r.at[j], (g, owner))

    def pass_x(j):
        @pl.loop(1, xs)
        def _(dx):
            landed(yrelay.at[j, dx - 1], y_r.at[j, dx - 1])
            send(yrelay.at[j, dx - 1], trecv.at[j, y_seq], f_s, t_r.at[j], (g, x_peer(dx) * 2 + yl))

    def cap_slot(group):
        return pl.ds(pl.multiple_of(group * cap_rows, cap_rows), cap_rows)

    def lanes_of(p):
        return pl.ds(PARCELS[p][1] * HD, PARCELS[p][2] * HD)

    def send_hi(p):
        i, first, count = PARCELS[p]
        for part in range(2):
            send(
                cap_ref.at[:, 1 - yh, :, :, pl.ds(col(hi_mine[i] + first + part * heads), count * HD)],
                hrelay.at[i, :, :, part, :, lanes_of(p)],
                h_s,
                h_r.at[p],
                hi_dev,
            )

    def send_z(p):
        i, first, count = PARCELS[p]

        @pl.loop(0, 2 * zs - 1)
        def _(n):
            pz, pc = z_peer(n)
            for part in range(2):
                send(
                    cap_ref.at[pz, yh, pc, :, pl.ds(col(mine[i] + first + part * heads), count * HD)],
                    capkv.at[i, part, cap_slot(g), lanes_of(p)],
                    c_s,
                    c_r.at[p],
                    ((pz * 2 + yh) * 2 + pc, s),
                )

    def own_z(i, part):
        return pltpu.make_async_copy(
            cap_ref.at[z, yh, core, :, pl.ds(col(mine[i] + part * heads), PAIR)],
            capkv.at[i, part, cap_slot(g)],
            local_sem.at[1 + chunks + 2 * i + part],
        )

    def own_pass(p):
        i = PARCELS[p][0]
        return pltpu.make_async_copy(
            hrelay.at[i, z, core, :, :, lanes_of(p)],
            capkv.at[i, :, cap_slot(hi_dev[0]), lanes_of(p)],
            local_sem.at[1 + chunks + 2 * SETS + p],
        )

    def pass_z(p):
        i = PARCELS[p][0]
        landed(hrelay.at[i, :, :, :, :, lanes_of(p)], h_r.at[p])

        @pl.loop(0, 2 * zs - 1)
        def _(n):
            pz, pc = z_peer(n)
            send(
                hrelay.at[i, pz, pc, :, :, lanes_of(p)],
                capkv.at[i, :, cap_slot(hi_dev[0]), lanes_of(p)],
                d_s,
                c_r.at[p],
                ((pz * 2 + yh) * 2 + pc, s),
            )

        own_pass(p).start()

    def own_t(j):
        return pltpu.make_async_copy(tq_ref.at[0, 0, spot_rows(s, j)], trecv.at[j, s], local_sem.at[1 + j])

    for copy in counts:
        copy.wait()
    frame_total = fc_ref[0]
    caption_total = cl_ref[0]

    def spatial(first, count):
        @pl.loop(first, first + count)
        def _(h):
            q, k, v = (spv[:, pl.ds(col(part * heads + h), HD)] for part in range(3))
            acc[:, pl.ds(col(h), HD)] = attend(q, k, v)

    def temporal(j):
        own_t(j).wait()
        landed(trecv.at[j, pl.ds(0, seqs - 1)], t_r.at[j])
        size = seqs * ROWS_T
        row = lax.broadcasted_iota(jnp.int32, (size, size), 0)
        column = lax.broadcasted_iota(jnp.int32, (size, size), 1)
        keep = ((row % ROWS_T) == (column % ROWS_T)) & (column // ROWS_T < frame_total)

        @pl.loop(0, heads // UNROLL)
        def _(n):
            for u in range(UNROLL):
                h = n * UNROLL + u
                q, k, v = (
                    trecv[j, :, :, pl.ds(col(part * heads + h), HD)].reshape(size, HD) for part in range(3)
                )
                mixed = attend_kept(q, k, v, keep)
                tsend[j, :, :, pl.ds(col(h), HD)] = mixed.astype(jnp.bfloat16).reshape(seqs, ROWS_T, HD)

        home = spot_rows(s, j)

        @pl.loop(1, xs)
        def _(dx):
            send(tsend.at[j, x_peer(dx) * 2 + 1 - yl], rrelay.at[j, dx - 1], b_s, b_r.at[j, dx - 1], (g, y_seq))

        send(tsend.at[j, y_seq], tret.at[home], b_s, r_r.at[j], (g, y_seq))

        tret[home] = tsend[j, s]

    def return_x(j):
        @pl.loop(1, xs)
        def _(dx):
            peer = x_peer(dx) * 2 + yl
            send(tsend.at[j, peer], tret.at[spot_rows(s, j)], a_s, r_r.at[j], (g, peer))

    def pass_back(j):
        @pl.loop(1, xs)
        def _(dx):
            landed(rrelay.at[j, dx - 1], b_r.at[j, dx - 1])
            send(rrelay.at[j, dx - 1], tret.at[spot_rows(y_seq, j)], g_s, r_r.at[j], (g, x_peer(dx) * 2 + yl))

    token = lax.broadcasted_iota(jnp.int32, (1, cap_tokens), 1)
    bias = jnp.where(token < caption_total, 0.0, NEG_FILL)

    def cross_theirs(p):
        i, first, count = PARCELS[p]
        if first == 0:
            landed(qpart.at[i], q_r.at[i])
            own_z(i, 0).wait()
            own_z(i, 1).wait()
        own_pass(p).wait()
        landed(capkv.at[i, :, pl.ds(0, cap_tokens - 2 * cap_rows), lanes_of(p)], c_r.at[p])

        @pl.loop(first, first + count)
        def _(k):
            lanes = pl.ds(col(k), HD)
            mixed = attend(qpart[i, :, lanes], capkv[i, 0, :, lanes], capkv[i, 1, :, lanes], bias)
            xsend[i, :, lanes] = mixed.astype(jnp.bfloat16)

    def send_cross(p):
        i = PARCELS[p][0]
        send(xsend.at[i, :, lanes_of(p)], xret.at[i, :, lanes_of(p)], x_s, x_r.at[p], (g, partners[i]))

    def cross_mine(p):
        i, first, count = PARCELS[p]

        @pl.loop(first, first + count)
        def _(k):
            lanes = pl.ds(col(k), HD)
            head = pl.ds(col(mine[i] + k), HD)
            acc[:, head] += attend(spv[:, head], capkv[i, 0, :, lanes], capkv[i, 1, :, lanes], bias)

    send_y(0)
    send_x(0)
    send_hi(0)
    send_y(1)
    send_x(1)
    send_hi(1)
    send_queries(0)
    send_queries(1)
    send_y(2)
    send_y(3)
    send_queries(2)
    send_hi(2)
    send_hi(3)
    for j in range(chunks):
        own_t(j).start()
    for i in range(SETS):
        own_z(i, 0).start()
        own_z(i, 1).start()
    wait_far()
    send_z(0)
    send_z(1)
    load_spatial.wait()
    spatial(0, 4)
    pass_x(0)
    send_x(2)
    pass_z(0)
    send_z(2)
    spatial(4, 4)
    pass_z(1)
    pass_x(1)
    send_x(3)
    send_z(3)
    temporal(0)
    pass_z(2)
    spatial(8, 2)
    pass_x(2)
    temporal(1)
    cross_theirs(0)
    pass_z(3)
    spatial(10, 2)
    pass_x(3)
    return_x(0)
    return_x(1)
    send_cross(0)
    temporal(2)
    return_x(2)
    cross_theirs(1)
    send_cross(1)
    pass_back(0)
    temporal(3)
    return_x(3)
    cross_mine(0)
    pass_back(1)
    cross_mine(1)
    cross_theirs(2)
    send_cross(2)
    pass_back(2)
    pass_back(3)
    cross_theirs(3)
    send_cross(3)
    cross_mine(2)
    cross_mine(3)

    keep_frame = (s + jnp.zeros((1, 1), jnp.int32)) < frame_total

    def write(rows, lanes, extra):
        total = acc[rows, lanes] + tret[rows, lanes].astype(jnp.float32)
        if extra is not None:
            total += extra
        out_ref[0, 0, rows, lanes] = jnp.where(keep_frame, total, 0.0).astype(jnp.bfloat16)

    *early, last = range(len(PARCELS))
    for p in early:
        i, first, count = PARCELS[p]
        landed(xret.at[i, :, lanes_of(p)], x_r.at[p])
        acc[:, pl.ds(col(theirs[i] + first), count * HD)] += xret[i, :, lanes_of(p)].astype(jnp.float32)
    last_set, last_head, _ = PARCELS[last]
    for j in range(chunks):
        landed(tret.at[pl.ds(0, (seqs - 1) * ROWS_T)], r_r.at[j])

        @pl.loop(0, seqs)
        def _(n):
            rows = spot_rows(n, j)
            for i in range(SETS):
                write(rows, pl.ds(col(mine[i]), PAIR), None)
                write(rows, pl.ds(col(theirs[i]), HD if i == last_set else PAIR), None)

    landed(xret.at[last_set, :, lanes_of(last)], x_r.at[last])
    write(pl.ds(0, tokens), pl.ds(col(theirs[last_set] + last_head), HD), xret[last_set, :, lanes_of(last)].astype(jnp.float32))

    landed(trecv.at[:, pl.ds(0, xs)], y_s)
    landed(trecv.at[:, pl.ds(0, xs - 1)], t_s)
    landed(yrelay, f_s)
    landed(tsend.at[:, pl.ds(0, xs)], b_s)
    landed(tsend.at[:, pl.ds(0, xs - 1)], a_s)
    landed(rrelay, g_s)
    landed(capkv.at[:, :, pl.ds(0, (2 * zs - 1) * cap_rows)], c_s)
    landed(capkv.at[:, :, pl.ds(0, (2 * zs - 1) * cap_rows)], d_s)
    landed(hrelay, h_s)
    landed(qpart, q_s)
    landed(xsend, x_s)


def body(dims, spatial_qkv, temporal_qkv, caption_kv, frame_count, caption_len):
    groups, seqs, tokens, feat = dims
    spots = tokens // seqs
    chunks = spots // ROWS_T
    cap_rows = caption_kv.shape[1]
    cap_tokens = groups * cap_rows
    caption_kv = caption_kv.reshape(groups // 4, 2, 2, cap_rows, 2 * feat)
    bf16 = jnp.bfloat16
    dma = pltpu.SemaphoreType.DMA
    return pl.pallas_call(
        functools.partial(kernel, dims),
        out_shape=pltpu.VMEM((1, 1, tokens, feat), bf16),
        in_specs=[pl.BlockSpec(memory_space=pl.ANY)] * 5,
        out_specs=pl.BlockSpec(memory_space=pltpu.VMEM),
        scratch_shapes=[
            pltpu.VMEM((tokens, 3 * feat), bf16),
            pltpu.VMEM((chunks, seqs, ROWS_T, 3 * feat), bf16),
            pltpu.VMEM((chunks, seqs // 2 - 1, ROWS_T, 3 * feat), bf16),
            pltpu.VMEM((chunks, seqs, ROWS_T, feat), bf16),
            pltpu.VMEM((chunks, seqs // 2 - 1, ROWS_T, feat), bf16),
            pltpu.VMEM((tokens, feat), bf16),
            pltpu.VMEM((SETS, 2, cap_tokens, PAIR), bf16),
            pltpu.VMEM((SETS, groups // 4, 2, 2, cap_rows, PAIR), bf16),
            pltpu.VMEM((SETS, tokens, PAIR), bf16),
            pltpu.VMEM((SETS, tokens, PAIR), bf16),
            pltpu.VMEM((SETS, tokens, PAIR), bf16),
            pltpu.VMEM((tokens, feat), jnp.float32),
            pltpu.SMEM((1,), jnp.int32),
            pltpu.SMEM((1,), jnp.int32),
            pltpu.SemaphoreType.REGULAR,
            pltpu.SemaphoreType.REGULAR,
            dma((2,)),
            dma((1 + chunks + 2 * SETS + len(PARCELS),)),
            dma, dma((chunks, seqs // 2 - 1)),
            dma, dma, dma((chunks,)),
            dma, dma, dma((chunks, seqs // 2 - 1)), dma, dma((chunks,)),
            dma, dma((len(PARCELS),)),
            dma, dma, dma((len(PARCELS),)),
            dma, dma((SETS,)),
            dma, dma((len(PARCELS),)),
        ],
        compiler_params=pltpu.CompilerParams(
            collective_id=0, has_side_effects=True, vmem_limit_bytes=56 << 20
        ),
    )(frame_count, caption_len, spatial_qkv, temporal_qkv, caption_kv)


def solution(mesh):
    groups, seqs = mesh.shape["group"], mesh.shape["seq"]
    placed = (
        P("group", "seq", None, None),
        P("group", "seq", None, None),
        P(None, "group", None),
        P("group"),
        P("group"),
    )

    def whole(spatial_qkv, *rest):
        dims = (groups, seqs, spatial_qkv.shape[2], spatial_qkv.shape[3] // 3)
        return jax.shard_map(
            functools.partial(body, dims),
            mesh=mesh,
            in_specs=placed,
            out_specs=P("group", "seq", None, None),
            check_vma=False,
        )(spatial_qkv, *rest)

    return whole
```
